32 devices in a mesh: groups: 2 (over y), leaf: 4 (over z), rows: 2 (over x), rhs: 2 (over core).
Axes of the slice: x: 2, y: 2, z: 4, core: 2. Of those that a mesh axis runs over, the one named last changes fastest.
Arguments:
- rhs: float32 [7168, 768], P(('groups', 'leaf', 'rows'), 'rhs'), parts along dimension 0, may hold values from -6 to 6
- dinv: float32 [7168, 512], P(('groups', 'leaf'), 'rows'), parts along dimension 0, may hold values from -3 to 3
- lower: float32 [10240, 512], P(('groups', 'leaf'), 'rows'), parts along dimension 0, may hold values from -0.25 to 0.25
- pattern: int32 [8, 3], P(('groups', 'leaf')), parts along dimension 0, may hold values 0 or 1
Outputs:
- solution: float32 [7168, 768], P(('groups', 'leaf', 'rows'), 'rhs'), parts along dimension 0
The draws below stay inside these ranges and needn't reach their ends.
There are 2 independent parts, one for each index of `groups`. The reference program is written for one: setup_inputs(seed, part) draws one part's arguments, and reference() takes and returns one part's arrays. A program takes and returns all parts, laid end to end along the dimension named above; each array names one. Nothing has to cross between parts.
All inputs are finite; a program needn't handle non-finite values. No bound on the sum of `pattern` on one device may be relied on, other than what follows from the above.
Results may differ from the reference program's by a relative error of at most 0.00015.
Values sent between devices are 32-bit elements; how exact they have to be, the bound alone decides.
A program may use at most 64 MiB of HBM per device.

```python
import math
import jax
import jax.numpy as jnp
from jax import lax

S = 512
LEAVES = 4
LEVELS = 2
ROW_SPLIT = 2
R = 768
PACK = 896
BP = 448
LPACK = 1280
NPAIR = 3


def draw_dinv(key, part):
    key = jax.random.fold_in(key, 11)
    row_ids = []
    for tree_level in range(LEVELS + 1):
        node_width = S >> tree_level
        position = (jnp.arange(LEAVES, dtype=jnp.int32) % 2 ** tree_level)[:, None] * node_width
        row_ids.append(position + jnp.arange(node_width, dtype=jnp.int32)[None, :])
    global_rows = jnp.concatenate(row_ids, axis=1).reshape(LEAVES * PACK)
    on_diag = (global_rows[:, None] == jnp.arange(S, dtype=jnp.int32)[None, :]).astype(jnp.float32)
    key_off, key_diag = jax.random.split(key, 2)
    spread = jax.random.truncated_normal(key_off, -4.0, 4.0, (LEAVES * PACK, S), jnp.float32)
    diagonal = jax.random.uniform(key_diag, (LEAVES * PACK, 1), jnp.float32, 0.8, 1.25)
    return on_diag * diagonal + 0.5 / math.sqrt(S) * spread


def draw_lower(key, part):
    key = jax.random.fold_in(key, 23)
    scales = []
    for tree_level in range(LEVELS):
        for upper_level in range(tree_level + 1, LEVELS + 1):
            factor = 0.6 / math.sqrt(S * 2 ** (upper_level - tree_level))
            scales.append(jnp.full((S >> tree_level,), factor, jnp.float32))
    section_scale = jnp.tile(jnp.concatenate(scales), LEAVES)[:, None]
    key_entry = jax.random.fold_in(key, 0)
    entries = jax.random.truncated_normal(key_entry, -4.0, 4.0, (LEAVES * LPACK, S), jnp.float32)
    return section_scale * entries


def place_ends(values, stream_key, smallest, top_value):
    longest = values.shape.index(max(values.shape))
    spots = []
    for shift in (0, 1):
        where = [jax.random.randint(jax.random.fold_in(stream_key, axis), (), 0, length) for axis, length in enumerate(values.shape)]
        where[longest] = (where[longest] + shift) % values.shape[longest]
        spots.append(tuple(where))
    return values.at[spots[0]].set(smallest).at[spots[1]].set(top_value)


def level_of(stream_key, dims, cuts, low, largest):
    gain = 1.0
    for dim, parts in cuts:
        heights = jax.random.uniform(jax.random.fold_in(jax.random.fold_in(stream_key, 6), dim), (parts,), jnp.float32, low / len(cuts), largest / len(cuts))
        gain = gain * jnp.repeat(jnp.exp(heights), dims[dim] // parts).reshape((-1,) + (1,) * (len(dims) - 1 - dim))
    return gain


def centred(stream_key, dims, width, bound, cuts=(), kind=jnp.bfloat16):
    loudness = level_of(stream_key, dims, cuts, -0.22, 0.18) if cuts else 1.0
    values = jax.random.normal(stream_key, dims, jnp.float32) * width * loudness
    return jnp.minimum(jnp.maximum(values, -bound), bound).astype(kind)


def setup_inputs(seed: int = 0, part: int = 0) -> dict:
    splits = jax.random.split(jax.random.key(seed), 5)
    part_splits = jax.random.split(jax.random.fold_in(splits[4], part), 5)
    return {
        "rhs": centred(part_splits[0], (LEAVES * ROW_SPLIT * BP, R), 1.0, 6.0, ((0, 8), (1, 2)), jnp.float32),
        "dinv": draw_dinv(jax.random.fold_in(jax.random.fold_in(splits[4], part), 71), part),
        "lower": draw_lower(jax.random.fold_in(jax.random.fold_in(splits[4], part), 71), part),
        "pattern": place_ends((jax.random.randint(part_splits[3], (LEAVES, NPAIR), 0, 4) < 3).astype(jnp.int32), jax.random.fold_in(part_splits[3], 1), 0, 1),
    }


def reference(rhs, dinv, lower, pattern):
    highest = lax.Precision.HIGHEST
    inverse_all = dinv.reshape(LEAVES, PACK, S)
    lower_all = lower.reshape(LEAVES, LPACK, S)
    rhs_all = rhs.reshape(LEAVES, ROW_SPLIT, BP, R)
    inverses = []
    sources = []
    offset = 0
    rhs_offset = 0
    for tree_level in range(LEVELS + 1):
        node_width = S >> tree_level
        node_span = 2 ** tree_level
        groups = LEAVES // node_span
        row_share = node_width // ROW_SPLIT
        inverses.append(inverse_all[:, offset:offset + node_width, :].reshape(groups, S, S))
        piece_rows = rhs_all[:, :, rhs_offset:rhs_offset + row_share, :].reshape(groups, node_span, ROW_SPLIT, row_share, R)
        sources.append(piece_rows.transpose(0, 2, 1, 3, 4).reshape(groups, S, R))
        offset += node_width
        rhs_offset += row_share
    couplings = {}
    lower_offset = 0
    section = 0
    for tree_level in range(LEVELS):
        node_width = S >> tree_level
        groups = LEAVES >> tree_level
        for upper_level in range(tree_level + 1, LEVELS + 1):
            keep_block = pattern[:, section].astype(jnp.float32)[:, None, None]
            block_rows = lower_all[:, lower_offset:lower_offset + node_width, :] * keep_block
            couplings[(tree_level, upper_level)] = block_rows.reshape(groups, S, S)
            lower_offset += node_width
            section += 1
    pending = [jnp.zeros((LEAVES >> tree_level, S, R), jnp.float32) for tree_level in range(LEVELS + 1)]
    solved = []
    for tree_level in range(LEVELS + 1):
        reduced = sources[tree_level] - pending[tree_level]
        current = jnp.einsum("giq,gqr->gir", inverses[tree_level], reduced, precision=highest)
        solved.append(current)
        for upper_level in range(tree_level + 1, LEVELS + 1):
            update = jnp.einsum("gis,gir->gsr", couplings[(tree_level, upper_level)], current, precision=highest)
            update = update.reshape(LEAVES >> upper_level, 2 ** (upper_level - tree_level), S, R).sum(axis=1)
            pending[upper_level] = pending[upper_level] + update
    answers = [None] * (LEVELS + 1)
    for tree_level in reversed(range(LEVELS + 1)):
        remainder = solved[tree_level]
        for upper_level in range(tree_level + 1, LEVELS + 1):
            spread_answer = jnp.repeat(answers[upper_level], 2 ** (upper_level - tree_level), axis=0)
            remainder = remainder - jnp.einsum("gis,gsr->gir", couplings[(tree_level, upper_level)], spread_answer, precision=highest)
        answers[tree_level] = jnp.einsum("giq,gir->gqr", inverses[tree_level], remainder, precision=highest)
    pieces = []
    for tree_level in range(LEVELS + 1):
        node_span = 2 ** tree_level
        groups = LEAVES // node_span
        row_share = (S >> tree_level) // ROW_SPLIT
        packed = answers[tree_level].reshape(groups, ROW_SPLIT, node_span, row_share, R).transpose(0, 2, 1, 3, 4)
        pieces.append(packed.reshape(LEAVES, ROW_SPLIT, row_share, R))
    return jnp.concatenate(pieces, axis=2).reshape(LEAVES * ROW_SPLIT * BP, R)
```

```python
import jax
import jax.numpy as jnp
from jax import lax
from jax.experimental import pallas as pl
from jax.experimental.pallas import tpu as pltpu
from jax.sharding import PartitionSpec as P

S = 512


def partner(value, axis, distance):
    mask = 2**distance
    pairs = [(source, source ^ mask) for source in range(lax.axis_size(axis))]
    return lax.ppermute(value, axis, pairs)


def subtree_total(summand, tree_depth):
    for bit_index in range(tree_depth):
        summand = summand + partner(summand, "leaf", bit_index)
    return summand


def contract_rows(matrix, vectors):
    return lax.dot_general(
        matrix,
        vectors,
        (((0,), (0,)), ((), ())),
        precision=lax.Precision.HIGHEST,
        preferred_element_type=jnp.float32,
    )


def body(rhs, dinv, lower, pattern):
    highest = lax.Precision.HIGHEST
    levels = lax.axis_size("leaf").bit_length() - 1
    row_split = lax.axis_size("rows")
    leaf_index = lax.axis_index("leaf")
    row_block = dinv.shape[1]
    rhs_cols = rhs.shape[1]
    block_masks = pattern[0].astype(jnp.float32)
    widths = [S >> tree_level for tree_level in range(levels + 1)]
    inverse_offsets = []
    offset = 0
    for node_width in widths:
        inverse_offsets.append(offset)
        offset += node_width
    sections = {}
    lower_offset = 0
    section = 0
    for tree_level in range(levels):
        for upper_level in range(tree_level + 1, levels + 1):
            sections[tree_level, upper_level] = (lower_offset, section)
            lower_offset += widths[tree_level]
            section += 1
    pending = [jnp.zeros((row_block, rhs_cols), jnp.float32) for tree_level in range(levels + 1)]
    solved = []
    for tree_level in range(levels + 1):
        node_width = widths[tree_level]
        row_share = node_width // row_split
        rhs_offset = inverse_offsets[tree_level] // row_split
        first_row = leaf_index % (1 << tree_level) * row_share
        own_rows = rhs[rhs_offset : rhs_offset + row_share]
        padded = lax.dynamic_update_slice_in_dim(
            jnp.zeros((row_block, rhs_cols), jnp.float32), own_rows, first_row, 0
        )
        reduced = subtree_total(padded - pending[tree_level], tree_level)
        inverse_block = dinv[inverse_offsets[tree_level] : inverse_offsets[tree_level] + node_width]
        local_product = jnp.dot(
            inverse_block, reduced, precision=highest, preferred_element_type=jnp.float32
        )
        solved_part = lax.psum(local_product, "rows")
        solved.append(solved_part)
        for upper_level in range(tree_level + 1, levels + 1):
            start_row, index_pair = sections[tree_level, upper_level]
            coupling = lower[start_row : start_row + node_width]
            pending[upper_level] = pending[upper_level] + block_masks[index_pair] * contract_rows(
                coupling, solved_part
            )
    answers = [None] * (levels + 1)
    for tree_level in reversed(range(levels + 1)):
        node_width = widths[tree_level]
        remainder = solved[tree_level]
        if tree_level < levels:
            partial_value = jnp.zeros((node_width, rhs_cols), jnp.float32)
            for upper_level in range(tree_level + 1, levels + 1):
                start_row, index_pair = sections[tree_level, upper_level]
                coupling = lower[start_row : start_row + node_width]
                partial_value = partial_value + block_masks[index_pair] * jnp.dot(
                    coupling,
                    answers[upper_level],
                    precision=highest,
                    preferred_element_type=jnp.float32,
                )
            remainder = remainder - lax.psum(partial_value, "rows")
        inverse_block = dinv[inverse_offsets[tree_level] : inverse_offsets[tree_level] + node_width]
        answers[tree_level] = subtree_total(contract_rows(inverse_block, remainder), tree_level)
    pieces = []
    for tree_level in range(levels + 1):
        row_share = widths[tree_level] // row_split
        first_row = leaf_index % (1 << tree_level) * row_share
        pieces.append(lax.dynamic_slice_in_dim(answers[tree_level], first_row, row_share, 0))
    return jnp.concatenate(pieces, axis=0)


F32 = jnp.float32
NT = (((1,), (1,)), ((), ()))
NN = (((1,), (0,)), ((), ()))


def split_two(a):
    hi = a.astype(jnp.bfloat16)
    return hi, (a - hi.astype(F32)).astype(jnp.bfloat16)


def dot3(a, b, dims):
    ah, al = split_two(a)
    bh, bl = split_two(b)
    one = lambda u, v: lax.dot_general(u, v, dims, preferred_element_type=F32)
    return one(ah, bh) + (one(ah, bl) + one(al, bh))


def kernel(
    rhs_ref, dinv_ref, lower_ref, pat_ref, out_ref,
    xd, xl, b12, zd, zl, d2, turned, rturned, y0, e1, e2, g1, g2, y1, g3, f2,
    s2, v1, v2, v0, ot, send_sem, recv_sem,
):
    r = lax.axis_index("rows")
    j = lax.axis_index("leaf")
    k = lax.axis_index("rhs")
    b0, b1 = j % 2, j // 2
    z0 = j + 1 - 2 * b0
    z1 = (j + 2) % 4
    z3 = (z0 + 2) % 4
    xp, kp = {"rows": 1 - r}, {"rhs": 1 - k}
    Z0, Z1, Z3 = {"leaf": z0}, {"leaf": z1}, {"leaf": z3}
    barrier = pltpu.get_barrier_semaphore()
    for peer in (xp, kp, Z0, Z1, Z3):
        pl.semaphore_signal(barrier, inc=1, device_id=peer, device_id_type=pl.DeviceIdType.MESH)
    pl.semaphore_wait(barrier, 5)

    sent = []

    def send(src, dst, peer):
        n = len(sent)
        copy = pltpu.make_async_remote_copy(
            src_ref=src, dst_ref=dst, send_sem=send_sem.at[n], recv_sem=recv_sem.at[n],
            device_id=peer, device_id_type=pl.DeviceIdType.MESH,
        )
        copy.start()
        sent.append(copy)
        return copy

    def part(start, rows):
        half = rows // 2
        return pl.ds(pl.multiple_of(start + k * half, 8), half)

    def hop(src, s_start, dst, d_start, rows, peer):
        return send(src.at[part(s_start, rows)], dst.at[part(d_start, rows)], peer)

    def share(copy, dst, d_start, rows):
        copy.wait_recv()
        return send(dst.at[part(d_start, rows)], dst.at[part(d_start, rows)], kp)

    h_d0 = hop(dinv_ref, 0, xd, 0, 512, xp)
    m01 = pat_ref[0, 0].astype(F32)
    m02 = pat_ref[0, 1].astype(F32)
    b12[0] = lower_ref[1024:1280] * pat_ref[0, 2].astype(F32)
    d2[0, 0:128] = dinv_ref[768:896]
    for c in range(0, 384, 128):
        for q in (0, 128, 256):
            turned[c : c + 128, q : q + 128] = rhs_ref[q : q + 128, c : c + 128].T
        last = rhs_ref[384:448, c : c + 128]
        turned[c : c + 128, 384:512] = jnp.concatenate([last, last], axis=0).T
    theirs = pl.ds(pl.multiple_of((1 - r) * 192, 8), 192)
    mine = pl.ds(pl.multiple_of(r * 192, 8), 192)
    q_a = send(turned.at[theirs, 0:256], rturned.at[:, 0:256], xp)
    h_b01 = hop(lower_ref, 0, xl, 0, 512, xp)
    z_d1 = hop(dinv_ref, 512, zd.at[0], 0, 256, Z0)
    z_b12 = hop(b12.at[0], 0, zl.at[0], 0, 256, Z0)
    h_d1 = hop(dinv_ref, 512, xd, 512, 256, xp)
    q_b = send(turned.at[theirs, 256:512], rturned.at[:, 256:512], xp)
    h_b02 = hop(lower_ref, 512, xl, 512, 512, xp)
    h_b12 = hop(b12.at[0], 0, b12.at[1], 0, 256, xp)
    h_d2 = hop(d2.at[0], 0, d2.at[1], 0, 128, xp)
    z_d2 = [hop(d2.at[0], 0, d2.at[0], 128 * (i + 1), 128, Z) for i, Z in enumerate((Z0, Z1, Z3))]

    s_d0 = share(h_d0, xd, 0, 512)
    q_a.wait_recv()
    y_own = dot3(turned[mine, 0:256], dinv_ref[0:512], NT)
    s_d0.wait_recv()
    y0[...] = y_own + dot3(rturned[:, 0:256], xd[0:512], NT)

    s_b01 = share(h_b01, xl, 0, 512)
    lane = lax.broadcasted_iota(jnp.int32, (192, 256), 1)
    q_b.wait_recv()

    def own_rows(h, level):
        v = (turned[mine, 256:512], rturned[:, 256:512])[h]
        v = v[:, 0:128] if level == 1 else v[:, 128:256]
        wide = jnp.concatenate([v, v], axis=1)
        where = (lane // 128 == b0) if level == 1 else (lane // 64 == j)
        return jnp.where(where, wide, 0.0)

    keep96 = pl.ds(pl.multiple_of(b0 * 96, 8), 96)
    give96 = pl.ds(pl.multiple_of((1 - b0) * 96, 8), 96)
    keep48 = pl.ds(pl.multiple_of(b1 * 48, 8), 48)
    give48 = pl.ds(pl.multiple_of((1 - b1) * 48, 8), 48)

    e1[0] = own_rows(0, 1) - m01 * dot3(y0[...], lower_ref[0:512], NN)
    s_b01.wait_recv()
    e1[1] = own_rows(1, 1) - m01 * dot3(y0[...], xl[0:512], NN)
    c_1 = send(e1.at[:, give96], g1, Z0)

    s_zd1 = share(z_d1, zd.at[0], 0, 256)
    s_d1 = share(h_d1, xd, 512, 256)
    z_xd1 = hop(xd, 512, zd.at[1], 0, 256, Z0)
    s_zb12 = share(z_b12, zl.at[0], 0, 256)
    e2[0] = own_rows(0, 2) - m02 * dot3(y0[...], lower_ref[512:1024], NN)
    s_b02 = share(h_b02, xl, 512, 512)
    s_xd1 = share(z_xd1, zd.at[1], 0, 256)
    s_b02.wait_recv()
    e2[1] = own_rows(1, 2) - m02 * dot3(y0[...], xl[512:1024], NN)
    c_2 = send(e2.at[:, give96], g2, Z0)
    s_b12 = share(h_b12, b12.at[1], 0, 256)
    z_xb12 = hop(b12.at[1], 0, zl.at[1], 0, 256, Z0)
    s_d2 = share(h_d2, d2.at[1], 0, 128)
    z_xd2 = [hop(d2.at[1], 0, d2.at[1], 128 * (i + 1), 128, Z) for i, Z in enumerate((Z0, Z1, Z3))]
    s_zd2 = [share(z, d2.at[0], 128 * (i + 1), 128) for i, z in enumerate(z_d2)]

    c_1.wait_recv()
    c1 = [e1[h, keep96] + g1[h] for h in range(2)]
    s_d1.wait_recv()
    y1[0] = dot3(c1[0], dinv_ref[512:768], NT) + dot3(c1[1], xd[512:768], NT)
    s_zd1.wait_recv()
    s_xd1.wait_recv()
    y1[1] = dot3(c1[0], zd[0], NT) + dot3(c1[1], zd[1], NT)
    s_xb12 = share(z_xb12, zl.at[1], 0, 256)
    s_zb12.wait_recv()
    s_b12.wait_recv()
    c_2.wait_recv()
    s_xb12.wait_recv()
    for h in range(2):
        up = dot3(y1[0], b12[h], NN) + dot3(y1[1], zl[h], NN)
        f2[h] = e2[h, keep96] + g2[h] - up
    c_3 = send(f2.at[:, give48], g3, Z1)
    s_xzd2 = [share(z, d2.at[1], 128 * (i + 1), 128) for i, z in enumerate(z_xd2)]

    for s in [s_d2] + s_zd2 + s_xzd2:
        s.wait_recv()
    c_3.wait_recv()
    y2 = dot3(f2[0, keep48] + g3[0], d2[0], NT) + dot3(f2[1, keep48] + g3[1], d2[1], NT)
    for h in range(2):
        s2[h] = dot3(y2, d2[h], NN)
    at48 = pl.ds(pl.multiple_of(b0 * 96 + b1 * 48, 8), 48)
    v2[:, at48] = s2[...]
    a_2 = send(s2, v2.at[:, at48], Z1)
    a_2.wait_recv()
    at96 = keep96
    b_2 = send(v2.at[:, at96], v2.at[:, at96], Z0)

    x2 = [v2[h, at96] for h in range(2)]
    r1 = [
        y1[0] - dot3(x2[0], b12[0], NT) - dot3(x2[1], b12[1], NT),
        y1[1] - dot3(x2[0], zl[0], NT) - dot3(x2[1], zl[1], NT),
    ]
    v1[0, at96] = dot3(r1[0], dinv_ref[512:768], NN) + dot3(r1[1], zd[0], NN)
    v1[1, at96] = dot3(r1[0], xd[512:768], NN) + dot3(r1[1], zd[1], NN)
    b_1 = send(v1.at[:, at96], v1.at[:, at96], Z0)
    b_2.wait_recv()
    l1 = pl.ds(pl.multiple_of(b0 * 128, 128), 128)
    l2 = pl.ds(pl.multiple_of(b1 * 128, 128), 128)
    o_2 = send(v2.at[1, :, l2], ot.at[mine, 384:512], xp)
    t = m02 * (dot3(v2[0], lower_ref[512:1024], NT) + dot3(v2[1], xl[512:1024], NT))
    y0[...] = y0[...] - t
    b_1.wait_recv()
    o_1 = send(v1.at[1, :, l1], ot.at[mine, 256:384], xp)

    t = m01 * (dot3(v1[0], lower_ref[0:512], NT) + dot3(v1[1], xl[0:512], NT))
    y0[...] = y0[...] - t
    v0[...] = dot3(y0[...], xd[0:512], NN)
    o_0 = send(v0, ot.at[mine, 0:256], xp)
    ot[mine, 0:256] = dot3(y0[...], dinv_ref[0:512], NN)
    ot[mine, 256:384] = v1[0, :, l1]
    ot[mine, 384:512] = v2[0, :, l2]
    o_2.wait_recv()
    o_1.wait_recv()
    for c in range(0, 384, 128):
        out_ref[256:384, c : c + 128] = ot[c : c + 128, 256:384].T
        both = ot[c : c + 128, 384:512].T
        out_ref[384:448, c : c + 128] = jnp.where(b0 == 0, both[0:64], both[64:128])
    o_0.wait_recv()
    for c in range(0, 384, 128):
        for q in (0, 128):
            out_ref[q : q + 128, c : c + 128] = ot[c : c + 128, q : q + 128].T
    for copy in sent:
        copy.wait_send()


MESSAGES = 64


def fused(rhs, dinv, lower, pattern):
    vm = lambda *shape: pltpu.VMEM(shape, F32)
    whole = pl.BlockSpec(memory_space=pltpu.VMEM)
    return pl.pallas_call(
        kernel,
        out_shape=jax.ShapeDtypeStruct(rhs.shape, F32),
        in_specs=[whole, whole, whole, pl.BlockSpec(memory_space=pltpu.SMEM)],
        out_specs=whole,
        scratch_shapes=[
            vm(896, 256), vm(1024, 256), vm(2, 256, 256), vm(2, 256, 256), vm(2, 256, 256),
            vm(2, 512, 256), vm(384, 512), vm(192, 512), vm(192, 512), vm(2, 192, 256),
            vm(2, 192, 256), vm(2, 96, 256), vm(2, 96, 256), vm(2, 96, 256), vm(2, 48, 256),
            vm(2, 96, 256), vm(2, 48, 256), vm(2, 192, 256), vm(2, 192, 256), vm(192, 256), vm(384, 512),
            pltpu.SemaphoreType.DMA((MESSAGES,)),
            pltpu.SemaphoreType.DMA((MESSAGES,)),
        ],
        compiler_params=pltpu.CompilerParams(
            collective_id=0, has_side_effects=True, vmem_limit_bytes=48 * 2**20
        ),
    )(rhs, dinv, lower, pattern)


def solution(mesh):
    sizes = mesh.shape
    small = sizes["leaf"] == 4 and sizes["rows"] == 2 and sizes["rhs"] == 2
    placed = (
        P(("groups", "leaf", "rows"), "rhs"),
        P(("groups", "leaf"), "rows"),
        P(("groups", "leaf"), "rows"),
        P(("groups", "leaf"), None),
    )
    return jax.shard_map(
        fused if small else body,
        mesh=mesh,
        in_specs=placed,
        out_specs=P(("groups", "leaf", "rows"), "rhs"),
        check_vma=False,
    )
```

```python
import jax
import jax.numpy as jnp
from jax import lax
from jax.experimental import pallas as pl
from jax.experimental.pallas import tpu as pltpu
from jax.sharding import PartitionSpec as P

S = 512


def partner(value, axis, distance):
    mask = 2**distance
    pairs = [(source, source ^ mask) for source in range(lax.axis_size(axis))]
    return lax.ppermute(value, axis, pairs)


def subtree_total(summand, tree_depth):
    for bit_index in range(tree_depth):
        summand = summand + partner(summand, "leaf", bit_index)
    return summand


def contract_rows(matrix, vectors):
    return lax.dot_general(
        matrix,
        vectors,
        (((0,), (0,)), ((), ())),
        precision=lax.Precision.HIGHEST,
        preferred_element_type=jnp.float32,
    )


def body(rhs, dinv, lower, pattern):
    highest = lax.Precision.HIGHEST
    levels = lax.axis_size("leaf").bit_length() - 1
    row_split = lax.axis_size("rows")
    leaf_index = lax.axis_index("leaf")
    row_block = dinv.shape[1]
    rhs_cols = rhs.shape[1]
    block_masks = pattern[0].astype(jnp.float32)
    widths = [S >> tree_level for tree_level in range(levels + 1)]
    inverse_offsets = []
    offset = 0
    for node_width in widths:
        inverse_offsets.append(offset)
        offset += node_width
    sections = {}
    lower_offset = 0
    section = 0
    for tree_level in range(levels):
        for upper_level in range(tree_level + 1, levels + 1):
            sections[tree_level, upper_level] = (lower_offset, section)
            lower_offset += widths[tree_level]
            section += 1
    pending = [jnp.zeros((row_block, rhs_cols), jnp.float32) for tree_level in range(levels + 1)]
    solved = []
    for tree_level in range(levels + 1):
        node_width = widths[tree_level]
        row_share = node_width // row_split
        rhs_offset = inverse_offsets[tree_level] // row_split
        first_row = leaf_index % (1 << tree_level) * row_share
        own_rows = rhs[rhs_offset : rhs_offset + row_share]
        padded = lax.dynamic_update_slice_in_dim(
            jnp.zeros((row_block, rhs_cols), jnp.float32), own_rows, first_row, 0
        )
        reduced = subtree_total(padded - pending[tree_level], tree_level)
        inverse_block = dinv[inverse_offsets[tree_level] : inverse_offsets[tree_level] + node_width]
        local_product = jnp.dot(
            inverse_block, reduced, precision=highest, preferred_element_type=jnp.float32
        )
        solved_part = lax.psum(local_product, "rows")
        solved.append(solved_part)
        for upper_level in range(tree_level + 1, levels + 1):
            start_row, index_pair = sections[tree_level, upper_level]
            coupling = lower[start_row : start_row + node_width]
            pending[upper_level] = pending[upper_level] + block_masks[index_pair] * contract_rows(
                coupling, solved_part
            )
    answers = [None] * (levels + 1)
    for tree_level in reversed(range(levels + 1)):
        node_width = widths[tree_level]
        remainder = solved[tree_level]
        if tree_level < levels:
            partial_value = jnp.zeros((node_width, rhs_cols), jnp.float32)
            for upper_level in range(tree_level + 1, levels + 1):
                start_row, index_pair = sections[tree_level, upper_level]
                coupling = lower[start_row : start_row + node_width]
                partial_value = partial_value + block_masks[index_pair] * jnp.dot(
                    coupling,
                    answers[upper_level],
                    precision=highest,
                    preferred_element_type=jnp.float32,
                )
            remainder = remainder - lax.psum(partial_value, "rows")
        inverse_block = dinv[inverse_offsets[tree_level] : inverse_offsets[tree_level] + node_width]
        answers[tree_level] = subtree_total(contract_rows(inverse_block, remainder), tree_level)
    pieces = []
    for tree_level in range(levels + 1):
        row_share = widths[tree_level] // row_split
        first_row = leaf_index % (1 << tree_level) * row_share
        pieces.append(lax.dynamic_slice_in_dim(answers[tree_level], first_row, row_share, 0))
    return jnp.concatenate(pieces, axis=0)


F32 = jnp.float32
NT = (((1,), (1,)), ((), ()))
NN = (((1,), (0,)), ((), ()))


def split_two(a):
    hi = a.astype(jnp.bfloat16)
    return hi, (a - hi.astype(F32)).astype(jnp.bfloat16)


def dot3(a, b, dims):
    ah, al = split_two(a)
    bh, bl = split_two(b)
    one = lambda u, v: lax.dot_general(u, v, dims, preferred_element_type=F32)
    return one(ah, bh) + (one(ah, bl) + one(al, bh))


def kernel(
    rhs_hbm, dinv_hbm, lower_hbm, pat_ref, out_ref,
    rhs_ref, dinv_ref, lower_ref, xd, xl, b12, zd, zl, d2, turned, rturned, y0, e1, e2,
    g1, g2, u1, u2, y1, g3, f2, s2, v1, v2, ob, ot, load_sem, send_sem, recv_sem,
):
    r = lax.axis_index("rows")
    j = lax.axis_index("leaf")
    k = lax.axis_index("rhs")
    b0, b1 = j % 2, j // 2
    z0 = j + 1 - 2 * b0
    z1 = (j + 2) % 4
    z3 = (z0 + 2) % 4
    xp, kp = {"rows": 1 - r}, {"rhs": 1 - k}
    Z0, Z1, Z3 = {"leaf": z0}, {"leaf": z1}, {"leaf": z3}
    barrier = pltpu.get_barrier_semaphore()
    for peer in (xp, kp, Z0, Z1, Z3):
        pl.semaphore_signal(barrier, inc=1, device_id=peer, device_id_type=pl.DeviceIdType.MESH)
    loads = [
        pltpu.make_async_copy(src, dst, load_sem.at[n])
        for n, (src, dst) in enumerate(
            ((rhs_hbm, rhs_ref), (dinv_hbm, dinv_ref), (lower_hbm, lower_ref))
        )
    ]
    for load in loads:
        load.start()
    pl.semaphore_wait(barrier, 5)

    sent = []

    def send(src, dst, peer):
        n = len(sent)
        copy = pltpu.make_async_remote_copy(
            src_ref=src, dst_ref=dst, send_sem=send_sem.at[n], recv_sem=recv_sem.at[n],
            device_id=peer, device_id_type=pl.DeviceIdType.MESH,
        )
        copy.start()
        sent.append(copy)
        return copy

    def part(start, rows):
        half = rows // 2
        return pl.ds(pl.multiple_of(start + k * half, 8), half)

    def hop(src, s_start, dst, d_start, rows, peer):
        return send(src.at[part(s_start, rows)], dst.at[part(d_start, rows)], peer)

    def share(copy, dst, d_start, rows):
        copy.wait_recv()
        return send(dst.at[part(d_start, rows)], dst.at[part(d_start, rows)], kp)

    def rows_at(start, size):
        return pl.ds(pl.multiple_of(start, 8), size)

    keep192, give192 = rows_at(b0 * 192, 192), rows_at((1 - b0) * 192, 192)
    keep96, give96 = rows_at(r * 96, 96), rows_at((1 - r) * 96, 96)
    keep48, give48 = rows_at(b1 * 48, 48), rows_at((1 - b1) * 48, 48)
    at96, off96 = rows_at(b0 * 96, 96), rows_at((1 - b0) * 96, 96)
    at48 = rows_at(b0 * 96 + b1 * 48, 48)

    h_d0 = hop(dinv_hbm, 0, xd, 0, 512, xp)
    loads[0].wait()
    for c in range(0, 384, 128):
        for q in (0, 128, 256):
            turned[c : c + 128, q : q + 128] = rhs_ref[q : q + 128, c : c + 128].T
        last = rhs_ref[384:448, c : c + 128]
        turned[c : c + 128, 384:512] = jnp.concatenate([last, last], axis=0).T
    q_a = send(turned.at[give192, 0:256], rturned.at[give192], xp)
    q_b = send(turned.at[keep192, 0:256], rturned.at[keep192], xp)
    m01 = pat_ref[0, 0].astype(F32)
    m02 = pat_ref[0, 1].astype(F32)
    z_d1 = hop(dinv_hbm, 512, zd.at[0], 0, 256, Z0)
    loads[1].wait()
    loads[2].wait()
    b12[0] = lower_ref[1024:1280] * pat_ref[0, 2].astype(F32)
    d2[0, 0:128] = dinv_ref[768:896]
    z_b12 = hop(b12.at[0], 0, zl.at[0], 0, 256, Z0)
    z_d2 = [hop(d2.at[0], 0, d2.at[0], 128 * (i + 1), 128, Z) for i, Z in enumerate((Z0, Z1, Z3))]

    lane = lax.broadcasted_iota(jnp.int32, (192, 256), 1)

    def own_rows(half, level):
        v = turned[half, 256:384] if level == 1 else turned[half, 384:512]
        where = (lane // 128 == b0) if level == 1 else (lane // 64 == j)
        return jnp.where(where, jnp.concatenate([v, v], axis=1), 0.0)

    y0[give192] = dot3(turned[give192, 0:256], dinv_ref[0:512], NT)
    s_d0 = share(h_d0, xd, 0, 512)
    y0[keep192] = dot3(turned[keep192, 0:256], dinv_ref[0:512], NT)
    q_a.wait_recv()
    s_d0.wait_recv()
    y = y0[give192] + dot3(rturned[give192], xd[0:512], NT)
    y0[give192] = y
    e1[0] = own_rows(give192, 1) - m01 * dot3(y, lower_ref[0:512], NN)
    c_1 = send(e1.at[0], g1, Z0)
    e2[0] = own_rows(give192, 2) - m02 * dot3(y, lower_ref[512:1024], NN)
    c_2 = send(e2.at[0], g2, Z0)
    h_d1 = hop(dinv_hbm, 512, xd, 512, 256, xp)
    s_zd1 = share(z_d1, zd.at[0], 0, 256)
    s_zb12 = share(z_b12, zl.at[0], 0, 256)
    q_b.wait_recv()
    h_b12 = hop(b12.at[0], 0, b12.at[1], 0, 256, xp)
    y = y0[keep192] + dot3(rturned[keep192], xd[0:512], NT)
    y0[keep192] = y
    e1[1] = own_rows(keep192, 1) - m01 * dot3(y, lower_ref[0:512], NN)
    e2[1] = own_rows(keep192, 2) - m02 * dot3(y, lower_ref[512:1024], NN)
    s_d1 = share(h_d1, xd, 512, 256)
    z_xd1 = hop(xd, 512, zd.at[1], 0, 256, Z0)
    c_1.wait_recv()
    e1[1] = e1[1] + g1[...]
    t_1 = send(e1.at[1, give96], u1, xp)
    h_d2 = hop(d2.at[0], 0, d2.at[1], 0, 128, xp)
    s_b12 = share(h_b12, b12.at[1], 0, 256)
    z_xb12 = hop(b12.at[1], 0, zl.at[1], 0, 256, Z0)
    c_2.wait_recv()
    e2[1] = e2[1] + g2[...]
    t_2 = send(e2.at[1, give96], u2, xp)
    h_b02 = hop(lower_hbm, 512, xl, 512, 512, xp)
    h_b01 = hop(lower_hbm, 0, xl, 0, 512, xp)
    s_zd2 = [share(z, d2.at[0], 128 * (i + 1), 128) for i, z in enumerate(z_d2)]

    s_xd1 = share(z_xd1, zd.at[1], 0, 256)
    t_1.wait_recv()
    c1 = [e1[1, keep96], u1[...]]
    s_d1.wait_recv()
    y1[0] = dot3(c1[0], dinv_ref[512:768], NT) + dot3(c1[1], xd[512:768], NT)
    s_d2 = share(h_d2, d2.at[1], 0, 128)
    z_xd2 = [hop(d2.at[1], 0, d2.at[1], 128 * (i + 1), 128, Z) for i, Z in enumerate((Z0, Z1, Z3))]
    s_zd1.wait_recv()
    s_xd1.wait_recv()
    y1[1] = dot3(c1[0], zd[0], NT) + dot3(c1[1], zd[1], NT)
    s_xb12 = share(z_xb12, zl.at[1], 0, 256)
    s_zb12.wait_recv()
    t_2.wait_recv()
    f2[0] = e2[1, keep96] - dot3(y1[0], b12[0], NN) - dot3(y1[1], zl[0], NN)
    s_b12.wait_recv()
    s_xb12.wait_recv()
    f2[1] = u2[...] - dot3(y1[0], b12[1], NN) - dot3(y1[1], zl[1], NN)
    c_3 = send(f2.at[:, give48], g3, Z1)
    s_xzd2 = [share(z, d2.at[1], 128 * (i + 1), 128) for i, z in enumerate(z_xd2)]

    for s in [s_d2] + s_zd2 + s_xzd2:
        s.wait_recv()
    c_3.wait_recv()
    y2 = dot3(f2[0, keep48] + g3[0], d2[0], NT) + dot3(f2[1, keep48] + g3[1], d2[1], NT)
    for h in range(2):
        s2[h] = dot3(y2, d2[h], NN)
    a_2 = send(s2, v2.at[:, at48], Z1)
    b_2 = send(s2, v2.at[:, at48], Z0)
    v2[:, at48] = s2[...]
    s_b02 = share(h_b02, xl, 512, 512)
    a_2.wait_recv()
    other48 = rows_at(b0 * 96 + (1 - b1) * 48, 48)
    b_3 = send(v2.at[:, other48], v2.at[:, other48], Z0)

    x2 = [v2[h, at96] for h in range(2)]
    r1 = [
        y1[0] - dot3(x2[0], b12[0], NT) - dot3(x2[1], b12[1], NT),
        y1[1] - dot3(x2[0], zl[0], NT) - dot3(x2[1], zl[1], NT),
    ]
    v1[0, at96] = dot3(r1[0], dinv_ref[512:768], NN) + dot3(r1[1], zd[0], NN)
    v1[1, at96] = dot3(r1[0], xd[512:768], NN) + dot3(r1[1], zd[1], NN)
    b_1 = send(v1.at[:, at96], v1.at[:, at96], Z0)
    s_b01 = share(h_b01, xl, 0, 512)

    l1 = pl.ds(pl.multiple_of(b0 * 128, 128), 128)
    l2 = pl.ds(pl.multiple_of(b1 * 128, 128), 128)
    arriving = []

    def upper_out(n, block, rows):
        ob[n, :, 256:384] = v1[1, block, l1]
        ob[n, :, 384:512] = v2[1, block, l2]
        arriving.append(send(ob.at[n, :, 256:512], ot.at[rows, 256:512], xp))
        ot[rows, 256:384] = v1[0, block, l1]
        ot[rows, 384:512] = v2[0, block, l2]

    def lowest(n, block, rows):
        t2 = dot3(v2[0, block], lower_ref[512:1024], NT) + dot3(v2[1, block], xl[512:1024], NT)
        t1 = dot3(v1[0, block], lower_ref[0:512], NT) + dot3(v1[1, block], xl[0:512], NT)
        rest = y0[rows] - m02 * t2 - m01 * t1
        ob[n, :, 0:256] = dot3(rest, xd[0:512], NN)
        arriving.append(send(ob.at[n, :, 0:256], ot.at[rows, 0:256], xp))
        ot[rows, 0:256] = dot3(rest, dinv_ref[0:512], NN)

    near, far = rows_at(b0 * 192 + r * 96, 96), rows_at((1 - b0) * 192 + r * 96, 96)
    upper_out(0, at96, near)
    s_b02.wait_recv()
    s_b01.wait_recv()
    lowest(0, at96, near)
    b_2.wait_recv()
    b_3.wait_recv()
    b_1.wait_recv()
    upper_out(1, off96, far)
    lowest(1, off96, far)
    arriving[0].wait_recv()
    arriving[2].wait_recv()
    for c in range(0, 384, 128):
        out_ref[256:384, c : c + 128] = ot[c : c + 128, 256:384].T
        both = ot[c : c + 128, 384:512].T
        out_ref[384:448, c : c + 128] = jnp.where(b0 == 0, both[0:64], both[64:128])
    arriving[1].wait_recv()
    arriving[3].wait_recv()
    for c in range(0, 384, 128):
        for q in (0, 128):
            out_ref[q : q + 128, c : c + 128] = ot[c : c + 128, q : q + 128].T
    for copy in sent:
        copy.wait_send()


MESSAGES = 64


def fused(rhs, dinv, lower, pattern):
    vm = lambda *shape: pltpu.VMEM(shape, F32)
    whole = pl.BlockSpec(memory_space=pltpu.VMEM)
    hbm = pl.BlockSpec(memory_space=pltpu.HBM)
    return pl.pallas_call(
        kernel,
        out_shape=jax.ShapeDtypeStruct(rhs.shape, F32),
        in_specs=[hbm, hbm, hbm, pl.BlockSpec(memory_space=pltpu.SMEM)],
        out_specs=whole,
        scratch_shapes=[
            vm(448, 384), vm(896, 256), vm(1280, 256), vm(896, 256), vm(1024, 256),
            vm(2, 256, 256), vm(2, 256, 256), vm(2, 256, 256), vm(2, 512, 256), vm(384, 512),
            vm(384, 256), vm(384, 512), vm(2, 192, 256), vm(2, 192, 256), vm(192, 256),
            vm(192, 256), vm(96, 256), vm(96, 256), vm(2, 96, 256), vm(2, 48, 256),
            vm(2, 96, 256), vm(2, 48, 256), vm(2, 192, 256), vm(2, 192, 256), vm(2, 96, 512),
            vm(384, 512),
            pltpu.SemaphoreType.DMA((3,)),
            pltpu.SemaphoreType.DMA((MESSAGES,)),
            pltpu.SemaphoreType.DMA((MESSAGES,)),
        ],
        compiler_params=pltpu.CompilerParams(
            collective_id=0, has_side_effects=True, vmem_limit_bytes=48 * 2**20
        ),
    )(rhs, dinv, lower, pattern)


def solution(mesh):
    sizes = mesh.shape
    small = sizes["leaf"] == 4 and sizes["rows"] == 2 and sizes["rhs"] == 2
    placed = (
        P(("groups", "leaf", "rows"), "rhs"),
        P(("groups", "leaf"), "rows"),
        P(("groups", "leaf"), "rows"),
        P(("groups", "leaf"), None),
    )
    return jax.shard_map(
        fused if small else body,
        mesh=mesh,
        in_specs=placed,
        out_specs=P(("groups", "leaf", "rows"), "rhs"),
        check_vma=False,
    )
```

```python
import jax
import jax.numpy as jnp
from jax import lax
from jax.experimental import pallas as pl
from jax.experimental.pallas import tpu as pltpu
from jax.sharding import PartitionSpec as P

S = 512


def partner(value, axis, distance):
    mask = 2**distance
    pairs = [(source, source ^ mask) for source in range(lax.axis_size(axis))]
    return lax.ppermute(value, axis, pairs)


def subtree_total(summand, tree_depth):
    for bit_index in range(tree_depth):
        summand = summand + partner(summand, "leaf", bit_index)
    return summand


def contract_rows(matrix, vectors):
    return lax.dot_general(
        matrix,
        vectors,
        (((0,), (0,)), ((), ())),
        precision=lax.Precision.HIGHEST,
        preferred_element_type=jnp.float32,
    )


def body(rhs, dinv, lower, pattern):
    highest = lax.Precision.HIGHEST
    levels = lax.axis_size("leaf").bit_length() - 1
    row_split = lax.axis_size("rows")
    leaf_index = lax.axis_index("leaf")
    row_block = dinv.shape[1]
    rhs_cols = rhs.shape[1]
    block_masks = pattern[0].astype(jnp.float32)
    widths = [S >> tree_level for tree_level in range(levels + 1)]
    inverse_offsets = []
    offset = 0
    for node_width in widths:
        inverse_offsets.append(offset)
        offset += node_width
    sections = {}
    lower_offset = 0
    section = 0
    for tree_level in range(levels):
        for upper_level in range(tree_level + 1, levels + 1):
            sections[tree_level, upper_level] = (lower_offset, section)
            lower_offset += widths[tree_level]
            section += 1
    pending = [jnp.zeros((row_block, rhs_cols), jnp.float32) for tree_level in range(levels + 1)]
    solved = []
    for tree_level in range(levels + 1):
        node_width = widths[tree_level]
        row_share = node_width // row_split
        rhs_offset = inverse_offsets[tree_level] // row_split
        first_row = leaf_index % (1 << tree_level) * row_share
        own_rows = rhs[rhs_offset : rhs_offset + row_share]
        padded = lax.dynamic_update_slice_in_dim(
            jnp.zeros((row_block, rhs_cols), jnp.float32), own_rows, first_row, 0
        )
        reduced = subtree_total(padded - pending[tree_level], tree_level)
        inverse_block = dinv[inverse_offsets[tree_level] : inverse_offsets[tree_level] + node_width]
        local_product = jnp.dot(
            inverse_block, reduced, precision=highest, preferred_element_type=jnp.float32
        )
        solved_part = lax.psum(local_product, "rows")
        solved.append(solved_part)
        for upper_level in range(tree_level + 1, levels + 1):
            start_row, index_pair = sections[tree_level, upper_level]
            coupling = lower[start_row : start_row + node_width]
            pending[upper_level] = pending[upper_level] + block_masks[index_pair] * contract_rows(
                coupling, solved_part
            )
    answers = [None] * (levels + 1)
    for tree_level in reversed(range(levels + 1)):
        node_width = widths[tree_level]
        remainder = solved[tree_level]
        if tree_level < levels:
            partial_value = jnp.zeros((node_width, rhs_cols), jnp.float32)
            for upper_level in range(tree_level + 1, levels + 1):
                start_row, index_pair = sections[tree_level, upper_level]
                coupling = lower[start_row : start_row + node_width]
                partial_value = partial_value + block_masks[index_pair] * jnp.dot(
                    coupling,
                    answers[upper_level],
                    precision=highest,
                    preferred_element_type=jnp.float32,
                )
            remainder = remainder - lax.psum(partial_value, "rows")
        inverse_block = dinv[inverse_offsets[tree_level] : inverse_offsets[tree_level] + node_width]
        answers[tree_level] = subtree_total(contract_rows(inverse_block, remainder), tree_level)
    pieces = []
    for tree_level in range(levels + 1):
        row_share = widths[tree_level] // row_split
        first_row = leaf_index % (1 << tree_level) * row_share
        pieces.append(lax.dynamic_slice_in_dim(answers[tree_level], first_row, row_share, 0))
    return jnp.concatenate(pieces, axis=0)


F32 = jnp.float32
NT = (((1,), (1,)), ((), ()))
NN = (((1,), (0,)), ((), ()))


def split_two(a):
    hi = a.astype(jnp.bfloat16)
    return hi, (a - hi.astype(F32)).astype(jnp.bfloat16)


def dot3(a, b, dims):
    ah, al = split_two(a)
    bh, bl = split_two(b)
    one = lambda u, v: lax.dot_general(u, v, dims, preferred_element_type=F32)
    return one(ah, bh) + (one(ah, bl) + one(al, bh))


def kernel(
    rhs_hbm, dinv_hbm, lower_hbm, pat_ref, out_ref,
    rhs_ref, dinv_ref, lower_ref, xd, xl, b12, zd, zl, d2, turned, rturned, y0, e1, e2,
    g1, g2, u1, u2, y1, g3, f2, s2, v1, v2, ob, ot, load_sem, send_sem, recv_sem,
):
    r = lax.axis_index("rows")
    j = lax.axis_index("leaf")
    k = lax.axis_index("rhs")
    b0, b1 = j % 2, j // 2
    z0 = j + 1 - 2 * b0
    z1 = (j + 2) % 4
    z3 = (z0 + 2) % 4
    xp, kp = {"rows": 1 - r}, {"rhs": 1 - k}
    Z0, Z1, Z3 = {"leaf": z0}, {"leaf": z1}, {"leaf": z3}
    barrier = pltpu.get_barrier_semaphore()
    for peer in (xp, kp, Z0, Z1, Z3):
        pl.semaphore_signal(barrier, inc=1, device_id=peer, device_id_type=pl.DeviceIdType.MESH)
    loads = [
        pltpu.make_async_copy(src, dst, load_sem.at[n])
        for n, (src, dst) in enumerate(
            ((rhs_hbm, rhs_ref), (dinv_hbm, dinv_ref), (lower_hbm, lower_ref))
        )
    ]
    for load in loads:
        load.start()
    pl.semaphore_wait(barrier, 5)

    sent = []

    def send(src, dst, peer):
        n = len(sent)
        copy = pltpu.make_async_remote_copy(
            src_ref=src, dst_ref=dst, send_sem=send_sem.at[n], recv_sem=recv_sem.at[n],
            device_id=peer, device_id_type=pl.DeviceIdType.MESH,
        )
        copy.start()
        sent.append(copy)
        return copy

    def part(start, rows):
        half = rows // 2
        return pl.ds(pl.multiple_of(start + k * half, 8), half)

    def hop(src, s_start, dst, d_start, rows, peer):
        return send(src.at[part(s_start, rows)], dst.at[part(d_start, rows)], peer)

    def share(copy, dst, d_start, rows):
        copy.wait_recv()
        return send(dst.at[part(d_start, rows)], dst.at[part(d_start, rows)], kp)

    def rows_at(start, size):
        return pl.ds(pl.multiple_of(start, 8), size)

    keep192, give192 = rows_at(b0 * 192, 192), rows_at((1 - b0) * 192, 192)
    keep96, give96 = rows_at(r * 96, 96), rows_at((1 - r) * 96, 96)
    keep48, give48 = rows_at(b1 * 48, 48), rows_at((1 - b1) * 48, 48)
    at96, off96 = rows_at(b0 * 96, 96), rows_at((1 - b0) * 96, 96)
    at48 = rows_at(b0 * 96 + b1 * 48, 48)

    h_d0 = hop(dinv_hbm, 0, xd, 0, 512, xp)
    loads[0].wait()
    for c in range(0, 384, 128):
        for q in (0, 128, 256):
            turned[c : c + 128, q : q + 128] = rhs_ref[q : q + 128, c : c + 128].T
        last = rhs_ref[384:448, c : c + 128]
        turned[c : c + 128, 384:512] = jnp.concatenate([last, last], axis=0).T
    q_a = send(turned.at[give192, 0:256], rturned.at[give192], xp)
    q_b = send(turned.at[keep192, 0:256], rturned.at[keep192], xp)
    m01 = pat_ref[0, 0].astype(F32)
    m02 = pat_ref[0, 1].astype(F32)
    z_d1 = hop(dinv_hbm, 512, zd.at[0], 0, 256, Z0)
    loads[1].wait()
    loads[2].wait()
    b12[0] = lower_ref[1024:1280] * pat_ref[0, 2].astype(F32)
    d2[0, 0:128] = dinv_ref[768:896]
    z_b12 = hop(b12.at[0], 0, zl.at[0], 0, 256, Z0)
    h_d1 = hop(dinv_hbm, 512, xd, 512, 256, xp)
    h_b12 = hop(b12.at[0], 0, b12.at[1], 0, 256, xp)
    h_d2 = hop(d2.at[0], 0, d2.at[1], 0, 128, xp)
    z_d2 = [hop(d2.at[0], 0, d2.at[0], 128 * (i + 1), 128, Z) for i, Z in enumerate((Z0, Z1, Z3))]

    lane = lax.broadcasted_iota(jnp.int32, (192, 256), 1)

    def own_rows(half, level):
        v = turned[half, 256:384] if level == 1 else turned[half, 384:512]
        where = (lane // 128 == b0) if level == 1 else (lane // 64 == j)
        return jnp.where(where, jnp.concatenate([v, v], axis=1), 0.0)

    y0[give192] = dot3(turned[give192, 0:256], dinv_ref[0:512], NT)
    s_d0 = share(h_d0, xd, 0, 512)
    y0[keep192] = dot3(turned[keep192, 0:256], dinv_ref[0:512], NT)
    q_a.wait_recv()
    s_d0.wait_recv()
    y = y0[give192] + dot3(rturned[give192], xd[0:512], NT)
    y0[give192] = y
    e1[0] = own_rows(give192, 1) - m01 * dot3(y, lower_ref[0:512], NN)
    c_1 = send(e1.at[0], g1, Z0)
    e2[0] = own_rows(give192, 2) - m02 * dot3(y, lower_ref[512:1024], NN)
    c_2 = send(e2.at[0], g2, Z0)
    s_zd1 = share(z_d1, zd.at[0], 0, 256)
    s_zb12 = share(z_b12, zl.at[0], 0, 256)
    q_b.wait_recv()
    y = y0[keep192] + dot3(rturned[keep192], xd[0:512], NT)
    y0[keep192] = y
    e1[1] = own_rows(keep192, 1) - m01 * dot3(y, lower_ref[0:512], NN)
    e2[1] = own_rows(keep192, 2) - m02 * dot3(y, lower_ref[512:1024], NN)
    s_d1 = share(h_d1, xd, 512, 256)
    z_xd1 = hop(xd, 512, zd.at[1], 0, 256, Z0)
    c_1.wait_recv()
    e1[1] = e1[1] + g1[...]
    t_1 = send(e1.at[1, give96], u1, xp)
    s_b12 = share(h_b12, b12.at[1], 0, 256)
    z_xb12 = hop(b12.at[1], 0, zl.at[1], 0, 256, Z0)
    s_d2 = share(h_d2, d2.at[1], 0, 128)
    z_xd2 = [hop(d2.at[1], 0, d2.at[1], 128 * (i + 1), 128, Z) for i, Z in enumerate((Z0, Z1, Z3))]
    c_2.wait_recv()
    e2[1] = e2[1] + g2[...]
    t_2 = send(e2.at[1, give96], u2, xp)
    h_b02 = hop(lower_hbm, 512, xl, 512, 512, xp)
    h_b01 = hop(lower_hbm, 0, xl, 0, 512, xp)
    s_zd2 = [share(z, d2.at[0], 128 * (i + 1), 128) for i, z in enumerate(z_d2)]

    s_xd1 = share(z_xd1, zd.at[1], 0, 256)
    t_1.wait_recv()
    c1 = [e1[1, keep96], u1[...]]
    s_d1.wait_recv()
    y1[0] = dot3(c1[0], dinv_ref[512:768], NT) + dot3(c1[1], xd[512:768], NT)
    s_zd1.wait_recv()
    s_xd1.wait_recv()
    y1[1] = dot3(c1[0], zd[0], NT) + dot3(c1[1], zd[1], NT)
    s_xb12 = share(z_xb12, zl.at[1], 0, 256)
    s_zb12.wait_recv()
    t_2.wait_recv()
    f2[0] = e2[1, keep96] - dot3(y1[0], b12[0], NN) - dot3(y1[1], zl[0], NN)
    s_b12.wait_recv()
    s_xb12.wait_recv()
    f2[1] = u2[...] - dot3(y1[0], b12[1], NN) - dot3(y1[1], zl[1], NN)
    c_3 = send(f2.at[:, give48], g3, Z1)
    s_xzd2 = [share(z, d2.at[1], 128 * (i + 1), 128) for i, z in enumerate(z_xd2)]

    for s in [s_d2] + s_zd2 + s_xzd2:
        s.wait_recv()
    c_3.wait_recv()
    y2 = dot3(f2[0, keep48] + g3[0], d2[0], NT) + dot3(f2[1, keep48] + g3[1], d2[1], NT)
    for h in range(2):
        s2[h] = dot3(y2, d2[h], NN)
    a_2 = send(s2, v2.at[:, at48], Z1)
    b_2 = send(s2, v2.at[:, at48], Z0)
    v2[:, at48] = s2[...]
    s_b02 = share(h_b02, xl, 512, 512)
    a_2.wait_recv()
    other48 = rows_at(b0 * 96 + (1 - b1) * 48, 48)
    b_3 = send(v2.at[:, other48], v2.at[:, other48], Z0)

    x2 = [v2[h, at96] for h in range(2)]
    r1 = [
        y1[0] - dot3(x2[0], b12[0], NT) - dot3(x2[1], b12[1], NT),
        y1[1] - dot3(x2[0], zl[0], NT) - dot3(x2[1], zl[1], NT),
    ]
    v1[0, at96] = dot3(r1[0], dinv_ref[512:768], NN) + dot3(r1[1], zd[0], NN)
    v1[1, at96] = dot3(r1[0], xd[512:768], NN) + dot3(r1[1], zd[1], NN)
    b_1 = send(v1.at[:, at96], v1.at[:, at96], Z0)
    s_b01 = share(h_b01, xl, 0, 512)

    l1 = pl.ds(pl.multiple_of(b0 * 128, 128), 128)
    l2 = pl.ds(pl.multiple_of(b1 * 128, 128), 128)
    arriving = []

    def upper_out(n, block, rows):
        ob[n, :, 256:384] = v1[1, block, l1]
        ob[n, :, 384:512] = v2[1, block, l2]
        arriving.append(send(ob.at[n, :, 256:512], ot.at[rows, 256:512], xp))
        ot[rows, 256:384] = v1[0, block, l1]
        ot[rows, 384:512] = v2[0, block, l2]

    def lowest(n, block, rows):
        t2 = dot3(v2[0, block], lower_ref[512:1024], NT) + dot3(v2[1, block], xl[512:1024], NT)
        t1 = dot3(v1[0, block], lower_ref[0:512], NT) + dot3(v1[1, block], xl[0:512], NT)
        rest = y0[rows] - m02 * t2 - m01 * t1
        ob[n, :, 0:256] = dot3(rest, xd[0:512], NN)
        arriving.append(send(ob.at[n, :, 0:256], ot.at[rows, 0:256], xp))
        ot[rows, 0:256] = dot3(rest, dinv_ref[0:512], NN)

    near, far = rows_at(b0 * 192 + r * 96, 96), rows_at((1 - b0) * 192 + r * 96, 96)
    upper_out(0, at96, near)
    s_b02.wait_recv()
    s_b01.wait_recv()
    lowest(0, at96, near)
    b_2.wait_recv()
    b_3.wait_recv()
    b_1.wait_recv()
    upper_out(1, off96, far)
    lowest(1, off96, far)
    arriving[0].wait_recv()
    arriving[2].wait_recv()
    for c in range(0, 384, 128):
        out_ref[256:384, c : c + 128] = ot[c : c + 128, 256:384].T
        both = ot[c : c + 128, 384:512].T
        out_ref[384:448, c : c + 128] = jnp.where(b0 == 0, both[0:64], both[64:128])
    arriving[1].wait_recv()
    arriving[3].wait_recv()
    for c in range(0, 384, 128):
        for q in (0, 128):
            out_ref[q : q + 128, c : c + 128] = ot[c : c + 128, q : q + 128].T
    for copy in sent:
        copy.wait_send()


MESSAGES = 64


def fused(rhs, dinv, lower, pattern):
    vm = lambda *shape: pltpu.VMEM(shape, F32)
    whole = pl.BlockSpec(memory_space=pltpu.VMEM)
    hbm = pl.BlockSpec(memory_space=pltpu.HBM)
    return pl.pallas_call(
        kernel,
        out_shape=jax.ShapeDtypeStruct(rhs.shape, F32),
        in_specs=[hbm, hbm, hbm, pl.BlockSpec(memory_space=pltpu.SMEM)],
        out_specs=whole,
        scratch_shapes=[
            vm(448, 384), vm(896, 256), vm(1280, 256), vm(896, 256), vm(1024, 256),
            vm(2, 256, 256), vm(2, 256, 256), vm(2, 256, 256), vm(2, 512, 256), vm(384, 512),
            vm(384, 256), vm(384, 512), vm(2, 192, 256), vm(2, 192, 256), vm(192, 256),
            vm(192, 256), vm(96, 256), vm(96, 256), vm(2, 96, 256), vm(2, 48, 256),
            vm(2, 96, 256), vm(2, 48, 256), vm(2, 192, 256), vm(2, 192, 256), vm(2, 96, 512),
            vm(384, 512),
            pltpu.SemaphoreType.DMA((3,)),
            pltpu.SemaphoreType.DMA((MESSAGES,)),
            pltpu.SemaphoreType.DMA((MESSAGES,)),
        ],
        compiler_params=pltpu.CompilerParams(
            collective_id=0, has_side_effects=True, vmem_limit_bytes=62 * 2**20
        ),
    )(rhs, dinv, lower, pattern)


def solution(mesh):
    sizes = mesh.shape
    small = sizes["leaf"] == 4 and sizes["rows"] == 2 and sizes["rhs"] == 2
    placed = (
        P(("groups", "leaf", "rows"), "rhs"),
        P(("groups", "leaf"), "rows"),
        P(("groups", "leaf"), "rows"),
        P(("groups", "leaf"), None),
    )
    return jax.shard_map(
        fused if small else body,
        mesh=mesh,
        in_specs=placed,
        out_specs=P(("groups", "leaf", "rows"), "rhs"),
        check_vma=False,
    )
```
